32 devices in a mesh: groups: 2 (over x), seq: 16 (over z, y, core).
Axes of the slice: x: 2, y: 2, z: 4, core: 2. Of those that a mesh axis runs over, the one named last changes fastest.
Arguments:
- mixer_in: bfloat16 [2048, 4608], P(('groups', 'seq')), parts along dimension 0, may hold values from -6 to 6
- gate_in: bfloat16 [2048, 4096], P(('groups', 'seq')), parts along dimension 0, may hold values from -6 to 6
- step_raw: bfloat16 [2048, 64], P(('groups', 'seq')), parts along dimension 0, may hold values from -3 to 3
- step_bias: float32 [64], replicated, may hold values from -1.5 to 0
- rate_log: float32 [64], replicated, as said below
- conv_weight: float32 [4, 4608], replicated, may hold values from -3 to 3
- conv_bias: float32 [4608], replicated, may hold values from -0.5 to 0.5
- skip_gain: float32 [64], replicated, may hold values from 0.5 to 1.5
- norm_gain: float32 [4096], replicated, may hold values from 0.1 to 1.9
- doc_lengths: int32 [12], P('groups'), parts along dimension 0, may hold values from 1 to 512, 1024 in all
Outputs:
- mixed_out: bfloat16 [2048, 4096], P(('groups', 'seq')), parts along dimension 0
The draws below stay inside these ranges and needn't reach their ends.
There are 2 independent parts, one for each index of `groups`. The reference program is written for one: setup_inputs(seed, part) draws one part's arguments, and reference() takes and returns one part's arrays. A program takes and returns all parts, laid end to end along the dimension named above; an argument that names none is the same for every part. Nothing has to cross between parts.
Inputs may be any that keep to these rules, and one draw needn't show every extreme that they name: `doc_lengths`: the 6 lengths of a part sum to 1024, and the longest is exactly 512. exp(rate_log) lies between 0.3 / 1024 and 0.08.
All inputs are finite; a program needn't handle non-finite values.
Results may differ from the reference program's by a relative error of at most 0.0043.
Values may be sent and summed in bfloat16 or wider, within the bound.
A program may use at most 320 MiB of HBM per device.

```python
import math
import jax
import jax.numpy as jnp
import numpy as np
from jax import lax

HEADS = 64
HEAD_DIM = 64
STATE = 64
GROUPS = 4
CONV = 4
DOCS = 6
TOK_DEV = 64
TOKENS = 1024
INNER = 4096
CH = 4608
DOC_MOST = 512
N_SEQ = 16


def draw_rate_log(key, part):
    chosen_key, levels_key = jax.random.split(jax.random.fold_in(key, 17))
    chosen = jax.random.randint(chosen_key, (HEADS,), 0, 10)
    levels = jax.random.uniform(levels_key, (HEADS,), jnp.float32)
    slow_mark = chosen < 5
    slow_low = math.log(0.3 / TOKENS)
    slow_high = math.log(3.0 / TOKENS)
    fast_low = math.log(0.01)
    fast_high = math.log(0.08)
    slow_part = slow_low + levels * (slow_high - slow_low)
    fast_part = fast_low + levels * (fast_high - fast_low)
    return jnp.where(slow_mark, slow_part, fast_part).astype(jnp.float32)


def steps_of(stream_key, extent, shards, low, high):
    level = 1.0
    for position, blocks in shards:
        heights = jax.random.uniform(jax.random.fold_in(jax.random.fold_in(stream_key, 6), position), (blocks,), jnp.float32, low / len(shards), high / len(shards))
        level = level * jnp.repeat(jnp.exp(heights), extent[position] // blocks).reshape((-1,) + (1,) * (len(extent) - 1 - position))
    return level


def length_profile(amount, total, reach, lean):
    weights = [(1 << 20) // math.isqrt(standing ** lean) + 1 for standing in range(2, amount + 1)]
    rest, given = total - reach - (amount - 1), [1] * (amount - 1)
    while rest > 0:
        movable = [i for i in range(amount - 1) if given[i] < reach]
        whole, remaining = sum([weights[i] for i in movable]), rest
        for i in movable:
            more = min(reach - given[i], max(1, remaining * weights[i] // whole), rest)
            given[i] = given[i] + more
            rest = rest - more
    return np.array([reach] + given)


def uneven_parts(rng, number_of, total, bound, skew):
    if number_of == 2:
        one = jax.random.randint(rng, (), max(1, total - bound), min(bound, total - 1) + 1)
        return jnp.stack([one, total - one])
    tallies = jnp.asarray(length_profile(number_of, total, bound, skew), jnp.int32)
    couples = (number_of - 1) // 2
    donor, sink = tallies[1:1 + 2 * couples:2], tallies[2:2 + 2 * couples:2]
    margin = jnp.minimum(donor - 1, bound - sink)
    shifted = jax.random.randint(jax.random.fold_in(rng, 1), (couples,), 0, 1 << 20) % (margin + 1)
    tallies = tallies.at[1:1 + 2 * couples:2].set(donor - shifted).at[2:2 + 2 * couples:2].set(sink + shifted)
    return tallies[jax.random.permutation(jax.random.fold_in(rng, 2), number_of)]


def noise(own_key, extent, width, bound, shards=(), held_as=jnp.bfloat16):
    gain = steps_of(own_key, extent, shards, -0.22, 0.18) if shards else 1.0
    drawn = jax.random.normal(own_key, extent, jnp.float32) * width * gain
    return jnp.minimum(jnp.maximum(drawn, -bound), bound).astype(held_as)


def setup_inputs(seed: int = 0, part: int = 0) -> dict:
    arg_keys = jax.random.split(jax.random.key(seed), 11)
    part_splits = jax.random.split(jax.random.fold_in(arg_keys[10], part), 11)
    return {
        "mixer_in": noise(part_splits[0], (TOKENS, CH), 1.0, 6.0, ((0, 16),)),
        "gate_in": noise(part_splits[1], (TOKENS, INNER), 1.0, 6.0, ((0, 16),)),
        "step_raw": noise(part_splits[2], (TOKENS, HEADS), 0.5, 3.0, ((0, 16),)),
        "step_bias": jnp.clip(jax.random.uniform(arg_keys[3], (HEADS,), jnp.float32, -1.5, 0.0), -1.5, 0.0),
        "rate_log": draw_rate_log(jax.random.fold_in(arg_keys[10], 71), part),
        "conv_weight": noise(arg_keys[5], (CONV, CH), CONV ** -0.5, 3.0, (), jnp.float32),
        "conv_bias": jnp.clip(jax.random.uniform(arg_keys[6], (CH,), jnp.float32, -0.5, 0.5), -0.5, 0.5),
        "skip_gain": jnp.clip(jax.random.uniform(arg_keys[7], (HEADS,), jnp.float32, 0.5, 1.5), 0.5, 1.5),
        "norm_gain": jnp.clip(1.0 + 0.18 * jax.random.normal(arg_keys[8], (INNER,), jnp.float32), 0.1, 1.9),
        "doc_lengths": uneven_parts(part_splits[9], DOCS, TOKENS, DOC_MOST, 2).astype(jnp.int32),
    }


epsilon = 1e-05

def doc_index(doc_lengths, positions):
    doc_ends = jnp.cumsum(doc_lengths).astype(jnp.int32)
    inside = lax.optimization_barrier(jnp.sum((positions[:, None] >= doc_ends[None, :]).astype(jnp.int32), axis=1))
    return jnp.where(positions >= 0, inside, -1).astype(jnp.int32)

def convolve(tok_block, rim_rows, positions, doc_lengths, conv_weight, conv_bias):
    rim_width = rim_rows.shape[0]
    length = tok_block.shape[0]
    padded = jnp.concatenate([rim_rows, tok_block], axis=0).astype(jnp.float32)
    all_positions = jnp.concatenate([positions[:rim_width] - rim_width, positions]).astype(jnp.int32)
    doc_ids = doc_index(doc_lengths, all_positions)
    own_doc = doc_ids[rim_width:]
    summed = jnp.zeros(tok_block.shape, jnp.float32) + conv_bias[None, :]
    for offset in range(rim_width + 1):
        same_doc = (doc_ids[offset:offset + length] == own_doc)[:, None]
        summed = summed + conv_weight[offset][None, :] * jnp.where(same_doc, padded[offset:offset + length], 0.0)
    return (jax.nn.silu(summed).astype(jnp.bfloat16), own_doc, doc_ids[rim_width - 1])

def group_terms(conv_x, conv_b, conv_c, step_size, log_sums, own_doc, prior_doc, skip_gain, member, group_heads, state_size):
    length = conv_x.shape[0]
    head_size = conv_x.shape[1] // skip_gain.shape[0]
    first = member * group_heads
    picked = slice(first, first + group_heads)
    x_group = conv_x[:, first * head_size:(first + group_heads) * head_size].reshape(length, group_heads, head_size).astype(jnp.float32)
    b_group = conv_b[:, member * state_size:(member + 1) * state_size]
    c_group = conv_c[:, member * state_size:(member + 1) * state_size]
    scores = jnp.dot(c_group, b_group.T, preferred_element_type=jnp.float32)
    places = jnp.arange(length, dtype=jnp.int32)
    causal = (places[:, None] >= places[None, :]) & (own_doc[:, None] == own_doc[None, :])
    head_logs = log_sums[:, picked].T
    log_gaps = head_logs[:, :, None] - head_logs[:, None, :]
    decays = jnp.exp(jnp.where(causal[None], log_gaps, -jnp.inf))
    head_steps = step_size[:, picked].T
    weights = (decays * scores[None] * head_steps[:, None, :]).astype(jnp.bfloat16)
    weights = lax.optimization_barrier(weights).astype(jnp.float32)
    within = jnp.einsum('hts,shp->thp', weights, x_group)
    within = within + skip_gain[picked][None, :, None] * x_group
    final_log = log_sums[-1, picked]
    tail_scale = jnp.exp(final_log[None, :] - log_sums[:, picked]) * step_size[:, picked] * (own_doc == own_doc[-1]).astype(jnp.float32)[:, None]
    weighted = (x_group * tail_scale[:, :, None]).astype(jnp.bfloat16)
    weighted = lax.optimization_barrier(weighted).astype(jnp.float32)
    local_state = jnp.einsum('shp,sn->hpn', weighted, b_group.astype(jnp.float32))
    inward = jnp.exp(log_sums[:, picked]) * (own_doc == prior_doc).astype(jnp.float32)[:, None]
    passing = jnp.exp(final_log) * (own_doc[-1] == prior_doc).astype(jnp.float32)
    return (within, local_state, inward, passing)

def carry_term(c_group, state_in, inward):
    rounded = lax.optimization_barrier(state_in.astype(jnp.bfloat16)).astype(jnp.float32)
    term = jnp.einsum('tn,hpn->thp', c_group.astype(jnp.float32), rounded)
    return term * inward[:, :, None]

def finish(mixed_out, gate_rows, norm_gain):
    length, head_count, head_size = mixed_out.shape
    gated = mixed_out * jax.nn.silu(gate_rows.astype(jnp.float32)).reshape(length, head_count, head_size)
    inv_rms = lax.rsqrt(lax.optimization_barrier(jnp.mean(gated * gated, axis=2, keepdims=True)) + epsilon)
    return ((gated * inv_rms).reshape(length, head_count * head_size) * norm_gain[None, :]).astype(jnp.bfloat16)

def reference(mixer_in, gate_in, step_raw, step_bias, rate_log, conv_weight, conv_bias, skip_gain, norm_gain, doc_lengths):
    rim_width = CONV - 1
    inner_width = HEADS * HEAD_DIM
    group_heads = HEADS // GROUPS

    def advance(carried, block_at):
        state_in, rim_rows = carried
        first_row = (block_at * TOK_DEV).astype(jnp.int32)
        tok_block = lax.dynamic_slice_in_dim(mixer_in, first_row, TOK_DEV, 0)
        gate_rows = lax.dynamic_slice_in_dim(gate_in, first_row, TOK_DEV, 0)
        raw_steps = lax.dynamic_slice_in_dim(step_raw, first_row, TOK_DEV, 0)
        positions = first_row + jnp.arange(TOK_DEV, dtype=jnp.int32)
        mixed, own_doc, prior_doc = convolve(tok_block, rim_rows, positions, doc_lengths, conv_weight, conv_bias)
        mixed = lax.optimization_barrier(mixed)
        conv_x = mixed[:, :inner_width]
        conv_b = mixed[:, inner_width:inner_width + GROUPS * STATE]
        conv_c = mixed[:, inner_width + GROUPS * STATE:]
        step_size = jax.nn.softplus(raw_steps.astype(jnp.float32) + step_bias[None, :])
        log_sums = jnp.cumsum(-jnp.exp(rate_log)[None, :] * step_size, axis=0)
        results = []
        new_states = []
        for member in range(GROUPS):
            within, local_state, inward, passing = group_terms(conv_x, conv_b, conv_c, step_size, log_sums, own_doc, prior_doc, skip_gain, member, group_heads, STATE)
            upper_state = state_in[member * group_heads:(member + 1) * group_heads]
            results.append(within + carry_term(conv_c[:, member * STATE:(member + 1) * STATE], upper_state, inward))
            new_states.append(passing[:, None, None] * upper_state + local_state)
        mixed_out = jnp.concatenate(results, axis=1)
        return ((jnp.concatenate(new_states, axis=0), tok_block[TOK_DEV - rim_width:]), finish(mixed_out, gate_rows, norm_gain))
    initial = (jnp.zeros((HEADS, HEAD_DIM, STATE), jnp.float32), jnp.zeros((rim_width, mixer_in.shape[1]), jnp.bfloat16))
    _, blocks = lax.scan(advance, initial, jnp.arange(N_SEQ, dtype=jnp.int32))
    return blocks.reshape(TOKENS, inner_width)
```

```python
import functools

import jax
import jax.numpy as jnp
from jax import lax
from jax.experimental import pallas as pl
from jax.experimental.pallas import tpu as pltpu
from jax.sharding import PartitionSpec as P

GROUPS = 4
PIECES = 2
epsilon = 1e-05
f32 = jnp.float32
bf16 = jnp.bfloat16


def dot(a, b):
    return jnp.dot(a, b, preferred_element_type=f32)


def halves(v):
    high = v.astype(bf16)
    return high, (v - high.astype(f32)).astype(bf16)


def sigmoid(v):
    return 0.5 * jnp.tanh(0.5 * v) + 0.5


def kernel(
    n_seq,
    doc_ref,
    mix_ref,
    gate_ref,
    raw_ref,
    bias_ref,
    rate_ref,
    cw_ref,
    cb_ref,
    skip_ref,
    norm_ref,
    out_ref,
    pad,
    rim_out,
    rim_in,
    l_wide,
    r_wide,
    e_wide,
    pass_out,
    pass_in,
    b_end,
    score,
    c_in,
    x_s,
    xs_s,
    part_s,
    sg_s,
    a_out,
    a_in,
    ch_out,
    ch_in,
    s_out,
    s_in,
    rim_sem,
    pass_send,
    pass_recv,
    a_send,
    a_recv,
    ch_send,
    ch_recv,
    s_send,
    s_recv,
):
    rows, ch = mix_ref.shape
    inner = gate_ref.shape[1]
    heads = raw_ref.shape[1]
    head_dim = inner // heads
    state = (ch - inner) // (2 * GROUPS)
    width = inner // GROUPS
    taps = cw_ref.shape[0]
    docs = doc_ref.shape[0]
    tile = min(256, width)
    piece = width // PIECES
    span = ch // 4

    me = lax.axis_index("seq")
    r = lax.rem(me, GROUPS)
    z = me // GROUPS
    nz = n_seq // GROUPS
    slab = z * GROUPS
    others = [lax.rem(r + 2, 4), 3 - r, r + 1 - 2 * lax.rem(r, 2)]
    nxt, prv = lax.rem(me + 1, n_seq), lax.rem(me + n_seq - 1, n_seq)
    up, down = lax.rem(me + GROUPS, n_seq), lax.rem(me + n_seq - GROUPS, n_seq)

    barrier = pltpu.get_barrier_semaphore()
    near = [slab + o for o in others] + [nxt, prv, up, down]
    for d in near:
        pl.semaphore_signal(barrier, inc=1, device_id={"seq": d}, device_id_type=pl.DeviceIdType.MESH)

    def remote(src, dst, send, recv, to):
        return pltpu.make_async_remote_copy(
            src_ref=src,
            dst_ref=dst,
            send_sem=send,
            recv_sem=recv,
            device_id={"seq": to},
            device_id_type=pl.DeviceIdType.MESH,
        )

    tail = mix_ref[rows - 16 :, :].astype(f32)
    lines = [
        tail[16 - (taps - 1) + t : 16 - (taps - 1) + t + 1, i * span : (i + 1) * span]
        for t in range(taps - 1)
        for i in range(4)
    ]
    lines = lines + [jnp.zeros((16 - len(lines), span), f32)]
    rim_out[...] = jnp.concatenate(lines, axis=0).astype(bf16)
    pl.semaphore_wait(barrier, len(near))
    rim_copy = remote(rim_out, rim_in, rim_sem.at[0], rim_sem.at[1], nxt)
    rim_copy.start()

    ends = []
    total = jnp.int32(0)
    for d in range(docs):
        total = total + doc_ref[d]
        ends.append(total)

    def doc_of(pos):
        inside = jnp.zeros(pos.shape, jnp.int32)
        for end in ends:
            inside = inside + jnp.where(pos >= end, 1, 0)
        return jnp.where(pos >= 0, inside, -1)

    first = me * rows
    pos_col = first + lax.broadcasted_iota(jnp.int32, (rows, 1), 0)
    own = doc_of(pos_col)
    own_row = doc_of(first + lax.broadcasted_iota(jnp.int32, (1, rows), 1))
    prior = doc_of(jnp.full((1, 1), first - 1, jnp.int32))
    last = doc_of(jnp.full((1, 1), first + rows - 1, jnp.int32))
    tap_same = [doc_of(pos_col - (taps - 1 - t)) == own for t in range(taps - 1)]

    step = jnp.log(1.0 + jnp.exp(raw_ref[...].astype(f32) + bias_ref[...]))
    fall = -jnp.exp(rate_ref[...]) * step
    below = lax.broadcasted_iota(jnp.int32, (rows, rows), 0) >= lax.broadcasted_iota(jnp.int32, (rows, rows), 1)
    logs = jnp.dot(below.astype(f32), fall, preferred_element_type=f32, precision=lax.Precision.HIGHEST)
    l_small = jnp.exp(logs)
    r_small = jnp.exp(-logs) * step
    e_small = l_small[rows - 1 : rows, :]
    p_small = jnp.where(last == prior, e_small, 0.0)

    low8 = jnp.concatenate([e_small, p_small, skip_ref[...], jnp.zeros((5, heads), f32)], axis=0)
    stack = jnp.concatenate([l_small, r_small, low8, jnp.zeros((8, heads), f32)], axis=0)
    high = stack.astype(bf16)
    rest = stack - high.astype(f32)
    mid = rest.astype(bf16)
    lows = (rest - mid.astype(f32)).astype(bf16)
    gap = lax.broadcasted_iota(jnp.int32, (heads, tile), 0) - (
        lax.broadcasted_iota(jnp.int32, (heads, tile), 1) // head_dim
    )
    for c in range(inner // tile):
        spread = jnp.where(gap == c * (tile // head_dim), 1.0, 0.0).astype(bf16)
        wide = dot(high, spread) + dot(mid, spread) + dot(lows, spread)
        cols = slice(c * tile, (c + 1) * tile)
        l_wide[:, cols] = wide[:rows]
        r_wide[:, cols] = wide[rows : 2 * rows]
        e_wide[:, cols] = wide[2 * rows : 2 * rows + 8]

    for g in range(GROUPS):
        pass_out[g] = e_wide[:, g * width : (g + 1) * width]
    pass_copies = []
    for o in others:
        copy = remote(pass_out.at[o], pass_in.at[r], pass_send.at[o], pass_recv.at[r], slab + o)
        copy.start()
        pass_copies.append(copy)
    pass_in[r] = pass_out[r]

    pad[8:, :] = mix_ref[...].astype(f32)
    rim_copy.wait()
    rim = rim_in[...].astype(f32)
    for t in range(taps - 1):
        for i in range(4):
            row = 8 - (taps - 1) + t
            pad[row : row + 1, i * span : (i + 1) * span] = rim[t * 4 + i : t * 4 + i + 1, :]

    def conv(start, size):
        cols = pl.ds(start, size)
        acc = cb_ref[:, cols] + cw_ref[taps - 1 : taps, cols] * pad[8:, cols]
        for t in range(taps - 1):
            row = 8 - (taps - 1) + t
            acc = acc + cw_ref[t : t + 1, cols] * jnp.where(tap_same[t], pad[row : row + rows, cols], 0.0)
        return (acc * sigmoid(acc)).astype(bf16)

    bs = conv(inner, GROUPS * state)
    cs = conv(inner + GROUPS * state, GROUPS * state)
    mask = below & (own == own_row)
    to_end = own == last
    from_prior = own == prior
    for g in range(GROUPS):
        b_g = bs[:, g * state : (g + 1) * state]
        c_g = cs[:, g * state : (g + 1) * state]
        raw_score = lax.dot_general(c_g, b_g, (((1,), (1,)), ((), ())), preferred_element_type=f32)
        score[g] = jnp.where(mask, raw_score, 0.0).astype(bf16)
        c_in[g] = jnp.where(from_prior, c_g.astype(f32), 0.0).astype(bf16)
        b_end[g] = jnp.where(to_end, b_g.astype(f32), 0.0).T.astype(bf16)

    def local(g, dst):
        def body(i, _):
            at = pl.multiple_of(g * width + i * tile, tile)
            cols = pl.ds(at, tile)
            x = conv(at, tile)
            x_s[:, cols] = x
            xs = (x.astype(f32) * r_wide[:, cols]).astype(bf16)
            xs_s[:, cols] = xs
            made = dot(b_end[g], xs) * e_wide[0:1, cols]
            dst[:, pl.ds(pl.multiple_of(i * tile, tile), tile)] = made.astype(bf16)
            return 0

        lax.fori_loop(0, width // tile, body, 0)

    a_copies = []
    for o in others:
        local(o, a_out.at[o])
        copy = remote(a_out.at[o], a_in.at[r], a_send.at[o], a_recv.at[r], slab + o)
        copy.start()
        a_copies.append(copy)
    local(r, a_in.at[r])

    def inside(i, _):
        g = i // (width // tile)
        cols = pl.ds(pl.multiple_of(i * tile, tile), tile)
        part_s[:, cols] = l_wide[:, cols] * dot(score[g], xs_s[:, cols]) + e_wide[2:3, cols] * x_s[:, cols].astype(f32)
        gate = gate_ref[:, cols].astype(f32)
        sg_s[:, cols] = gate * sigmoid(gate)
        return 0

    lax.fori_loop(0, inner // tile, inside, 0)

    for o in others:
        remote(pass_out.at[o], pass_in.at[o], pass_send.at[o], pass_recv.at[o], slab + o).wait_recv()
        remote(a_out.at[o], a_in.at[o], a_send.at[o], a_recv.at[o], slab + o).wait_recv()

    for p in range(PIECES):
        cols = slice(p * piece, (p + 1) * piece)
        chain = remote(ch_out.at[p], ch_in.at[p], ch_send.at[p], ch_recv.at[p], up)

        @pl.when(z == 0)
        def _():
            ch_in[p] = jnp.zeros((state, piece), bf16)

        @pl.when(z > 0)
        def _():
            chain.wait_recv()

        held = ch_in[p].astype(f32)
        steps = []
        for k in range(GROUPS):
            steps.append(held)
            held = held * pass_in[k, 1:2, cols] + a_in[k, :, cols].astype(f32)
        ch_out[p] = held.astype(bf16)

        @pl.when(z < nz - 1)
        def _():
            chain.start()

        for k in range(GROUPS):
            s_out[k, p] = steps[k].astype(bf16)
        for o in others:
            remote(
                s_out.at[o, p], s_in.at[r, p], s_send.at[o * PIECES + p], s_recv.at[r * PIECES + p], slab + o
            ).start()
        s_in[r, p] = s_out[r, p]

    ones = jnp.where(
        lax.broadcasted_iota(jnp.int32, (tile, tile), 0) // head_dim
        == lax.broadcasted_iota(jnp.int32, (tile, tile), 1) // head_dim,
        1.0 / head_dim,
        0.0,
    ).astype(bf16)

    def finish(g, p):
        def body(i, _):
            cols = pl.ds(pl.multiple_of(g * width + p * piece + i * tile, tile), tile)
            arrived = s_in[g, p, :, pl.ds(pl.multiple_of(i * tile, tile), tile)]
            both = part_s[:, cols] + l_wide[:, cols] * dot(c_in[g], arrived)
            gated = both * sg_s[:, cols]
            sq_high, sq_low = halves(gated * gated)
            mean = dot(sq_high, ones) + dot(sq_low, ones)
            out_ref[:, cols] = (gated * lax.rsqrt(mean + epsilon) * norm_ref[:, cols]).astype(bf16)
            return 0

        lax.fori_loop(0, piece // tile, body, 0)

    for p in range(PIECES):
        finish(r, p)
        for o in [others[2], others[0], others[1]]:
            remote(
                s_out.at[o, p], s_in.at[o, p], s_send.at[o * PIECES + p], s_recv.at[o * PIECES + p], slab + o
            ).wait_recv()
            finish(o, p)

    for copy in pass_copies + a_copies:
        copy.wait_send()
    for p in range(PIECES):
        for o in others:
            remote(
                s_out.at[o, p], s_in.at[r, p], s_send.at[o * PIECES + p], s_recv.at[r * PIECES + p], slab + o
            ).wait_send()

        @pl.when(z < nz - 1)
        def _():
            remote(ch_out.at[p], ch_in.at[p], ch_send.at[p], ch_recv.at[p], up).wait_send()


def on_device(
    n_seq,
    mixer_in,
    gate_in,
    step_raw,
    step_bias,
    rate_log,
    conv_weight,
    conv_bias,
    skip_gain,
    norm_gain,
    doc_lengths,
):
    rows, ch = mixer_in.shape
    inner = gate_in.shape[1]
    heads = step_raw.shape[1]
    state = (ch - inner) // (2 * GROUPS)
    width = inner // GROUPS
    piece = width // PIECES
    vmem = pl.BlockSpec(memory_space=pltpu.VMEM)
    dma = pltpu.SemaphoreType.DMA
    return pl.pallas_call(
        functools.partial(kernel, n_seq),
        out_shape=jax.ShapeDtypeStruct((rows, inner), bf16),
        in_specs=[pl.BlockSpec(memory_space=pltpu.SMEM)] + [vmem] * 9,
        out_specs=vmem,
        scratch_shapes=[
            pltpu.VMEM((rows + 8, ch), f32),
            pltpu.VMEM((16, ch // 4), bf16),
            pltpu.VMEM((16, ch // 4), bf16),
            pltpu.VMEM((rows, inner), f32),
            pltpu.VMEM((rows, inner), f32),
            pltpu.VMEM((8, inner), f32),
            pltpu.VMEM((GROUPS, 8, width), f32),
            pltpu.VMEM((GROUPS, 8, width), f32),
            pltpu.VMEM((GROUPS, state, rows), bf16),
            pltpu.VMEM((GROUPS, rows, rows), bf16),
            pltpu.VMEM((GROUPS, rows, state), bf16),
            pltpu.VMEM((rows, inner), bf16),
            pltpu.VMEM((rows, inner), bf16),
            pltpu.VMEM((rows, inner), f32),
            pltpu.VMEM((rows, inner), f32),
            pltpu.VMEM((GROUPS, state, width), bf16),
            pltpu.VMEM((GROUPS, state, width), bf16),
            pltpu.VMEM((PIECES, state, piece), bf16),
            pltpu.VMEM((PIECES, state, piece), bf16),
            pltpu.VMEM((GROUPS, PIECES, state, piece), bf16),
            pltpu.VMEM((GROUPS, PIECES, state, piece), bf16),
            dma((2,)),
            dma((GROUPS,)),
            dma((GROUPS,)),
            dma((GROUPS,)),
            dma((GROUPS,)),
            dma((PIECES,)),
            dma((PIECES,)),
            dma((GROUPS * PIECES,)),
            dma((GROUPS * PIECES,)),
        ],
        compiler_params=pltpu.CompilerParams(
            collective_id=0, has_side_effects=True, vmem_limit_bytes=40 * 1024 * 1024
        ),
        cost_estimate=pl.CostEstimate(flops=100_000_000, bytes_accessed=2_000_000, transcendentals=1_000_000),
    )(
        doc_lengths,
        mixer_in,
        gate_in,
        step_raw,
        step_bias[None, :],
        rate_log[None, :],
        conv_weight,
        conv_bias[None, :],
        skip_gain[None, :],
        norm_gain[None, :],
    )


def solution(mesh):
    return jax.shard_map(
        functools.partial(on_device, mesh.shape["seq"]),
        mesh=mesh,
        in_specs=(
            P(("groups", "seq"), None),
            P(("groups", "seq"), None),
            P(("groups", "seq"), None),
            P(),
            P(),
            P(),
            P(),
            P(),
            P(),
            P("groups"),
        ),
        out_specs=P(("groups", "seq"), None),
        check_vma=False,
    )
```

```python
import functools

import jax
import jax.numpy as jnp
from jax import lax
from jax.experimental import pallas as pl
from jax.experimental.pallas import tpu as pltpu
from jax.sharding import PartitionSpec as P

GROUPS = 4
PIECES = 2
epsilon = 1e-05
f32 = jnp.float32
bf16 = jnp.bfloat16


def dot(a, b):
    return jnp.dot(a, b, preferred_element_type=f32)


def halves(v):
    high = v.astype(bf16)
    return high, (v - high.astype(f32)).astype(bf16)


def sigmoid(v):
    return 0.5 * jnp.tanh(0.5 * v) + 0.5


def nz_half(n_seq):
    return max(1, n_seq // GROUPS // 2)


def kernel(
    n_seq,
    doc_ref,
    mix_ref,
    gate_ref,
    raw_ref,
    bias_ref,
    rate_ref,
    cw_ref,
    cb_ref,
    skip_ref,
    norm_ref,
    out_ref,
    ext,
    gate_s,
    cw_s,
    cb_s,
    l_wide,
    r_wide,
    e_wide,
    pass_out,
    pass_in,
    b_end,
    score,
    c_in,
    x_s,
    xs_s,
    part_s,
    sg_s,
    a_out,
    a_in,
    ch_out,
    ch_in,
    s_out,
    s_in,
    load_sem,
    rim_sem,
    pass_send,
    pass_recv,
    a_send,
    a_recv,
    ch_send,
    ch_recv,
    s_send,
    s_recv,
):
    rows, ch = mix_ref.shape
    inner = gate_ref.shape[1]
    heads = raw_ref.shape[1]
    head_dim = inner // heads
    state = (ch - inner) // (2 * GROUPS)
    width = inner // GROUPS
    taps = cw_ref.shape[0]
    docs = doc_ref.shape[0]
    tile = min(256, width)
    piece = width // PIECES
    reach = nz_half(n_seq)

    me = lax.axis_index("seq")
    r = lax.rem(me, GROUPS)
    z = me // GROUPS
    nz = n_seq // GROUPS
    slab = z * GROUPS
    others = [lax.rem(r + 2, 4), 3 - r, r + 1 - 2 * lax.rem(r, 2)]
    nxt, prv = lax.rem(me + 1, n_seq), lax.rem(me + n_seq - 1, n_seq)
    up, down = lax.rem(me + GROUPS, n_seq), lax.rem(me + n_seq - GROUPS, n_seq)

    loads = [
        pltpu.make_async_copy(mix_ref, ext.at[pl.ds(0, rows)], load_sem.at[0]),
        pltpu.make_async_copy(cw_ref, cw_s, load_sem.at[1]),
        pltpu.make_async_copy(cb_ref, cb_s.at[0], load_sem.at[2]),
        pltpu.make_async_copy(gate_ref, gate_s, load_sem.at[3]),
    ]
    for load in loads:
        load.start()
    barrier = pltpu.get_barrier_semaphore()
    near = [slab + o for o in others] + [nxt, prv, up, down]
    for d in near:
        pl.semaphore_signal(barrier, inc=1, device_id={"seq": d}, device_id_type=pl.DeviceIdType.MESH)

    def remote(src, dst, send, recv, to):
        return pltpu.make_async_remote_copy(
            src_ref=src,
            dst_ref=dst,
            send_sem=send,
            recv_sem=recv,
            device_id={"seq": to},
            device_id_type=pl.DeviceIdType.MESH,
        )

    pl.semaphore_wait(barrier, len(near))
    loads[0].wait()
    rim_copy = remote(
        ext.at[pl.ds(rows - 16, 16)], ext.at[pl.ds(rows, 16)], rim_sem.at[0], rim_sem.at[1], nxt
    )
    rim_copy.start()

    ends = []
    total = jnp.int32(0)
    for d in range(docs):
        total = total + doc_ref[d]
        ends.append(total)

    def doc_of(pos):
        inside = jnp.zeros(pos.shape, jnp.int32)
        for end in ends:
            inside = inside + jnp.where(pos >= end, 1, 0)
        return jnp.where(pos >= 0, inside, -1)

    first = me * rows
    pos_col = first + lax.broadcasted_iota(jnp.int32, (rows, 1), 0)
    own = doc_of(pos_col)
    own_row = doc_of(first + lax.broadcasted_iota(jnp.int32, (1, rows), 1))
    prior = doc_of(jnp.full((1, 1), first - 1, jnp.int32))
    last = doc_of(jnp.full((1, 1), first + rows - 1, jnp.int32))
    tap_same = [doc_of(pos_col - (taps - 1 - t)) == own for t in range(taps - 1)]

    step = jnp.log(1.0 + jnp.exp(raw_ref[...].astype(f32) + bias_ref[...]))
    fall = -jnp.exp(rate_ref[...]) * step
    below = lax.broadcasted_iota(jnp.int32, (rows, rows), 0) >= lax.broadcasted_iota(jnp.int32, (rows, rows), 1)
    logs = jnp.dot(below.astype(f32), fall, preferred_element_type=f32, precision=lax.Precision.HIGHEST)
    l_small = jnp.exp(logs)
    r_small = jnp.exp(-logs) * step
    e_small = l_small[rows - 1 : rows, :]
    p_small = jnp.where(last == prior, e_small, 0.0)

    low8 = jnp.concatenate([e_small, p_small, skip_ref[...], jnp.zeros((5, heads), f32)], axis=0)
    stack = jnp.concatenate([l_small, r_small, low8, jnp.zeros((8, heads), f32)], axis=0)
    split = jnp.concatenate(halves(stack), axis=1)
    gap = lax.rem(lax.broadcasted_iota(jnp.int32, (2 * heads, tile), 0), heads) - (
        lax.broadcasted_iota(jnp.int32, (2 * heads, tile), 1) // head_dim
    )
    for c in range(inner // tile):
        wide = dot(split, jnp.where(gap == c * (tile // head_dim), 1.0, 0.0).astype(bf16))
        cols = slice(c * tile, (c + 1) * tile)
        l_wide[:, cols] = wide[:rows]
        r_wide[:, cols] = wide[rows : 2 * rows]
        e_wide[:, cols] = wide[2 * rows : 2 * rows + 8]

    for g in range(GROUPS):
        pass_out[g] = e_wide[:, g * width : (g + 1) * width]
    pass_copies = []
    for o in others:
        copy = remote(pass_out.at[o], pass_in.at[r], pass_send.at[o], pass_recv.at[r], slab + o)
        copy.start()
        pass_copies.append(copy)
    pass_in[r] = pass_out[r]

    place = lax.broadcasted_iota(jnp.int32, (rows, rows + 16), 1)
    place = jnp.where(place < rows, place, place - (rows + 16))
    behind = lax.broadcasted_iota(jnp.int32, (rows, rows + 16), 0) - place
    shift = jnp.concatenate(
        [jnp.where((behind == taps - 1 - t) & tap_same[t], 1.0, 0.0) for t in range(taps - 1)], axis=0
    ).astype(bf16)
    loads[1].wait()
    loads[2].wait()
    rim_copy.wait()

    def conv(start, size):
        cols = pl.ds(start, size)
        moved = dot(shift, ext[:, cols])
        acc = cb_s[:, cols] + cw_s[taps - 1 : taps, cols] * ext[:rows, cols].astype(f32)
        for t in range(taps - 1):
            acc = acc + cw_s[t : t + 1, cols] * moved[t * rows : (t + 1) * rows]
        return (acc * sigmoid(acc)).astype(bf16)

    bs = conv(inner, GROUPS * state)
    cs = conv(inner + GROUPS * state, GROUPS * state)
    mask = below & (own == own_row)
    to_end = own == last
    from_prior = own == prior
    for g in range(GROUPS):
        b_g = bs[:, g * state : (g + 1) * state]
        c_g = cs[:, g * state : (g + 1) * state]
        raw_score = lax.dot_general(c_g, b_g, (((1,), (1,)), ((), ())), preferred_element_type=f32)
        score[g] = jnp.where(mask, raw_score, 0.0).astype(bf16)
        c_in[g] = jnp.where(from_prior, c_g.astype(f32), 0.0).astype(bf16)
        b_end[g] = jnp.where(to_end, b_g.astype(f32), 0.0).T.astype(bf16)

    def local(g, dst):
        def body(i, _):
            at = pl.multiple_of(g * width + i * tile, tile)
            cols = pl.ds(at, tile)
            x = conv(at, tile)
            x_s[:, cols] = x
            xs = (x.astype(f32) * r_wide[:, cols]).astype(bf16)
            xs_s[:, cols] = xs
            made = dot(b_end[g], xs) * e_wide[0:1, cols]
            dst[:, pl.ds(pl.multiple_of(i * tile, tile), tile)] = made.astype(bf16)
            return 0

        lax.fori_loop(0, width // tile, body, 0, unroll=True)

    a_copies = []
    for o in others:
        local(o, a_out.at[o])
        copy = remote(a_out.at[o], a_in.at[r], a_send.at[o], a_recv.at[r], slab + o)
        copy.start()
        a_copies.append(copy)
    local(r, a_in.at[r])

    def inside(i, _):
        g = i // (width // tile)
        cols = pl.ds(pl.multiple_of(i * tile, tile), tile)
        part_s[:, cols] = l_wide[:, cols] * dot(score[g], xs_s[:, cols]) + e_wide[2:3, cols] * x_s[:, cols].astype(f32)
        gate = gate_s[:, cols].astype(f32)
        sg_s[:, cols] = gate * sigmoid(gate)
        return 0

    loads[3].wait()
    lax.fori_loop(0, inner // tile, inside, 0, unroll=True)

    for o in others:
        remote(pass_out.at[o], pass_in.at[o], pass_send.at[o], pass_recv.at[o], slab + o).wait_recv()
        remote(a_out.at[o], a_in.at[o], a_send.at[o], a_recv.at[o], slab + o).wait_recv()

    def chain(i, p):
        at = i * PIECES + p
        return remote(ch_out.at[at], ch_in.at[at], ch_send.at[at], ch_recv.at[at], up)

    def emit(p):
        cols = slice(p * piece, (p + 1) * piece)
        total = a_in[0, :, cols].astype(f32)
        for k in range(1, GROUPS):
            total = total * pass_in[k, 1:2, cols] + a_in[k, :, cols].astype(f32)
        ch_out[p] = total.astype(bf16)

        @pl.when(z < nz - 1)
        def _():
            chain(0, p).start()

    def gather(i, p):
        @pl.when(z == 0)
        def _():
            ch_in[i * PIECES + p] = jnp.zeros((state, piece), bf16)

        @pl.when(z > 0)
        def _():
            chain(i, p).wait_recv()

        if i + 1 < reach:
            cols = slice(p * piece, (p + 1) * piece)
            whole = pass_in[0, 1:2, cols]
            for k in range(1, GROUPS):
                whole = whole * pass_in[k, 1:2, cols]
            ch_out[(i + 1) * PIECES + p] = (ch_in[i * PIECES + p].astype(f32) * whole).astype(bf16)

            @pl.when(z < nz - 1)
            def _():
                chain(i + 1, p).start()

    for p in range(PIECES):
        emit(p)
    for i in range(reach - 1):
        for p in range(PIECES):
            gather(i, p)
    for p in range(PIECES):
        gather(reach - 1, p)
        cols = slice(p * piece, (p + 1) * piece)
        held = ch_in[p].astype(f32)
        for i in range(1, reach):
            held = held + ch_in[i * PIECES + p].astype(f32)
        for k in range(GROUPS):
            s_out[k, p] = held.astype(bf16)
            if k + 1 < GROUPS:
                held = held * pass_in[k, 1:2, cols] + a_in[k, :, cols].astype(f32)
        for o in others:
            remote(
                s_out.at[o, p], s_in.at[r, p], s_send.at[o * PIECES + p], s_recv.at[r * PIECES + p], slab + o
            ).start()
        s_in[r, p] = s_out[r, p]

    ones = jnp.where(
        lax.broadcasted_iota(jnp.int32, (tile, tile), 0) // head_dim
        == lax.broadcasted_iota(jnp.int32, (tile, tile), 1) // head_dim,
        1.0 / head_dim,
        0.0,
    ).astype(bf16)

    def finish(g, p):
        def body(i, _):
            cols = pl.ds(pl.multiple_of(g * width + p * piece + i * tile, tile), tile)
            arrived = s_in[g, p, :, pl.ds(pl.multiple_of(i * tile, tile), tile)]
            both = part_s[:, cols] + l_wide[:, cols] * dot(c_in[g], arrived)
            gated = both * sg_s[:, cols]
            mean = dot((gated * gated).astype(bf16), ones)
            out_ref[:, cols] = (gated * lax.rsqrt(mean + epsilon) * norm_ref[:, cols]).astype(bf16)
            return 0

        lax.fori_loop(0, piece // tile, body, 0, unroll=True)

    for p in range(PIECES):
        finish(r, p)
        for o in [others[2], others[0], others[1]]:
            remote(
                s_out.at[o, p], s_in.at[o, p], s_send.at[o * PIECES + p], s_recv.at[o * PIECES + p], slab + o
            ).wait_recv()
            finish(o, p)

    for copy in pass_copies + a_copies:
        copy.wait_send()
    for p in range(PIECES):
        for o in others:
            remote(
                s_out.at[o, p], s_in.at[r, p], s_send.at[o * PIECES + p], s_recv.at[r * PIECES + p], slab + o
            ).wait_send()

        for i in range(reach):

            @pl.when(z < nz - 1)
            def _():
                chain(i, p).wait_send()


def on_device(
    n_seq,
    mixer_in,
    gate_in,
    step_raw,
    step_bias,
    rate_log,
    conv_weight,
    conv_bias,
    skip_gain,
    norm_gain,
    doc_lengths,
):
    rows, ch = mixer_in.shape
    inner = gate_in.shape[1]
    heads = step_raw.shape[1]
    state = (ch - inner) // (2 * GROUPS)
    width = inner // GROUPS
    piece = width // PIECES
    vmem = pl.BlockSpec(memory_space=pltpu.VMEM)
    hbm = pl.BlockSpec(memory_space=pltpu.HBM)
    reach = nz_half(n_seq)
    dma = pltpu.SemaphoreType.DMA
    return pl.pallas_call(
        functools.partial(kernel, n_seq),
        out_shape=jax.ShapeDtypeStruct((rows, inner), bf16),
        in_specs=[pl.BlockSpec(memory_space=pltpu.SMEM), hbm, hbm] + [vmem] * 3 + [hbm, hbm] + [vmem] * 2,
        out_specs=vmem,
        scratch_shapes=[
            pltpu.VMEM((rows + 16, ch), bf16),
            pltpu.VMEM((rows, inner), bf16),
            pltpu.VMEM(conv_weight.shape, f32),
            pltpu.VMEM((1, ch), f32),
            pltpu.VMEM((rows, inner), f32),
            pltpu.VMEM((rows, inner), f32),
            pltpu.VMEM((8, inner), f32),
            pltpu.VMEM((GROUPS, 8, width), f32),
            pltpu.VMEM((GROUPS, 8, width), f32),
            pltpu.VMEM((GROUPS, state, rows), bf16),
            pltpu.VMEM((GROUPS, rows, rows), bf16),
            pltpu.VMEM((GROUPS, rows, state), bf16),
            pltpu.VMEM((rows, inner), bf16),
            pltpu.VMEM((rows, inner), bf16),
            pltpu.VMEM((rows, inner), f32),
            pltpu.VMEM((rows, inner), f32),
            pltpu.VMEM((GROUPS, state, width), bf16),
            pltpu.VMEM((GROUPS, state, width), bf16),
            pltpu.VMEM((reach * PIECES, state, piece), bf16),
            pltpu.VMEM((reach * PIECES, state, piece), bf16),
            pltpu.VMEM((GROUPS, PIECES, state, piece), bf16),
            pltpu.VMEM((GROUPS, PIECES, state, piece), bf16),
            dma((4,)),
            dma((2,)),
            dma((GROUPS,)),
            dma((GROUPS,)),
            dma((GROUPS,)),
            dma((GROUPS,)),
            dma((reach * PIECES,)),
            dma((reach * PIECES,)),
            dma((GROUPS * PIECES,)),
            dma((GROUPS * PIECES,)),
        ],
        compiler_params=pltpu.CompilerParams(
            collective_id=0, has_side_effects=True, vmem_limit_bytes=40 * 1024 * 1024
        ),
        cost_estimate=pl.CostEstimate(flops=100_000_000, bytes_accessed=2_000_000, transcendentals=1_000_000),
    )(
        doc_lengths,
        mixer_in,
        gate_in,
        step_raw,
        step_bias[None, :],
        rate_log[None, :],
        conv_weight,
        conv_bias,
        skip_gain[None, :],
        norm_gain[None, :],
    )


def solution(mesh):
    return jax.shard_map(
        functools.partial(on_device, mesh.shape["seq"]),
        mesh=mesh,
        in_specs=(
            P(("groups", "seq"), None),
            P(("groups", "seq"), None),
            P(("groups", "seq"), None),
            P(),
            P(),
            P(),
            P(),
            P(),
            P(),
            P("groups"),
        ),
        out_specs=P(("groups", "seq"), None),
        check_vma=False,
    )
```

```python
import functools

import jax
import jax.numpy as jnp
from jax import lax
from jax.experimental import pallas as pl
from jax.experimental.pallas import tpu as pltpu
from jax.sharding import PartitionSpec as P

GROUPS = 4
PIECES = 2
epsilon = 1e-05
f32 = jnp.float32
bf16 = jnp.bfloat16


def dot(a, b):
    return jnp.dot(a, b, preferred_element_type=f32)


def halves(v):
    high = v.astype(bf16)
    return high, (v - high.astype(f32)).astype(bf16)


def sigmoid(v):
    return 0.5 * jnp.tanh(0.5 * v) + 0.5


def nz_half(n_seq):
    return max(1, n_seq // GROUPS // 2)


def kernel(
    n_seq,
    doc_hbm,
    mix_ref,
    gate_ref,
    raw_hbm,
    bias_hbm,
    rate_hbm,
    cw_ref,
    cb_ref,
    skip_hbm,
    norm_hbm,
    out_ref,
    ext,
    gate_s,
    cw_s,
    cb_s,
    doc_ref,
    raw_ref,
    bias_ref,
    rate_ref,
    skip_ref,
    norm_ref,
    l_wide,
    r_wide,
    e_wide,
    pass_out,
    pass_in,
    b_end,
    score,
    c_in,
    x_s,
    xs_s,
    part_s,
    sg_s,
    a_out,
    a_in,
    ch_out,
    ch_in,
    s_out,
    s_in,
    load_sem,
    rim_sem,
    pass_send,
    pass_recv,
    a_send,
    a_recv,
    ch_send,
    ch_recv,
    s_send,
    s_recv,
):
    rows, ch = mix_ref.shape
    inner = gate_ref.shape[1]
    heads = raw_hbm.shape[1]
    head_dim = inner // heads
    state = (ch - inner) // (2 * GROUPS)
    width = inner // GROUPS
    taps = cw_ref.shape[0]
    docs = doc_hbm.shape[0]
    tile = min(256, width)
    piece = width // PIECES
    reach = nz_half(n_seq)

    me = lax.axis_index("seq")
    r = lax.rem(me, GROUPS)
    z = me // GROUPS
    nz = n_seq // GROUPS
    slab = z * GROUPS
    others = [lax.rem(r + 2, 4), 3 - r, r + 1 - 2 * lax.rem(r, 2)]
    nxt, prv = lax.rem(me + 1, n_seq), lax.rem(me + n_seq - 1, n_seq)
    up, down = lax.rem(me + GROUPS, n_seq), lax.rem(me + n_seq - GROUPS, n_seq)

    loads = [
        pltpu.make_async_copy(mix_ref, ext.at[pl.ds(0, rows)], load_sem.at[0]),
        pltpu.make_async_copy(cw_ref, cw_s, load_sem.at[1]),
        pltpu.make_async_copy(cb_ref, cb_s.at[0], load_sem.at[2]),
        pltpu.make_async_copy(gate_ref, gate_s, load_sem.at[3]),
        pltpu.make_async_copy(doc_hbm, doc_ref, load_sem.at[4]),
        pltpu.make_async_copy(raw_hbm, raw_ref, load_sem.at[5]),
        pltpu.make_async_copy(bias_hbm, bias_ref.at[0], load_sem.at[6]),
        pltpu.make_async_copy(rate_hbm, rate_ref.at[0], load_sem.at[7]),
        pltpu.make_async_copy(skip_hbm, skip_ref.at[0], load_sem.at[8]),
        pltpu.make_async_copy(norm_hbm, norm_ref.at[0], load_sem.at[9]),
    ]
    for load in loads:
        load.start()
    barrier = pltpu.get_barrier_semaphore()
    near = [slab + o for o in others] + [nxt, prv, up, down]
    for d in near:
        pl.semaphore_signal(barrier, inc=1, device_id={"seq": d}, device_id_type=pl.DeviceIdType.MESH)

    def remote(src, dst, send, recv, to):
        return pltpu.make_async_remote_copy(
            src_ref=src,
            dst_ref=dst,
            send_sem=send,
            recv_sem=recv,
            device_id={"seq": to},
            device_id_type=pl.DeviceIdType.MESH,
        )

    pl.semaphore_wait(barrier, len(near))
    loads[0].wait()
    rim_copy = remote(
        ext.at[pl.ds(rows - 16, 16)], ext.at[pl.ds(rows, 16)], rim_sem.at[0], rim_sem.at[1], nxt
    )
    rim_copy.start()

    for load in loads[4:]:
        load.wait()

    ends = []
    total = jnp.int32(0)
    for d in range(docs):
        total = total + doc_ref[d]
        ends.append(total)

    def doc_of(pos):
        inside = jnp.zeros(pos.shape, jnp.int32)
        for end in ends:
            inside = inside + jnp.where(pos >= end, 1, 0)
        return jnp.where(pos >= 0, inside, -1)

    first = me * rows
    pos_col = first + lax.broadcasted_iota(jnp.int32, (rows, 1), 0)
    own = doc_of(pos_col)
    own_row = doc_of(first + lax.broadcasted_iota(jnp.int32, (1, rows), 1))
    prior = doc_of(jnp.full((1, 1), first - 1, jnp.int32))
    last = doc_of(jnp.full((1, 1), first + rows - 1, jnp.int32))
    tap_same = [doc_of(pos_col - (taps - 1 - t)) == own for t in range(taps - 1)]

    step = jnp.log(1.0 + jnp.exp(raw_ref[...].astype(f32) + bias_ref[...]))
    fall = -jnp.exp(rate_ref[...]) * step
    below = lax.broadcasted_iota(jnp.int32, (rows, rows), 0) >= lax.broadcasted_iota(jnp.int32, (rows, rows), 1)
    logs = jnp.dot(below.astype(f32), fall, preferred_element_type=f32, precision=lax.Precision.HIGHEST)
    l_small = jnp.exp(logs)
    r_small = jnp.exp(-logs) * step
    e_small = l_small[rows - 1 : rows, :]
    p_small = jnp.where(last == prior, e_small, 0.0)

    low8 = jnp.concatenate([e_small, p_small, skip_ref[...], jnp.zeros((5, heads), f32)], axis=0)
    stack = jnp.concatenate([l_small, r_small, low8, jnp.zeros((8, heads), f32)], axis=0)
    split = jnp.concatenate(halves(stack), axis=1)
    gap = lax.rem(lax.broadcasted_iota(jnp.int32, (2 * heads, tile), 0), heads) - (
        lax.broadcasted_iota(jnp.int32, (2 * heads, tile), 1) // head_dim
    )
    for c in range(inner // tile):
        wide = dot(split, jnp.where(gap == c * (tile // head_dim), 1.0, 0.0).astype(bf16))
        cols = slice(c * tile, (c + 1) * tile)
        l_wide[:, cols] = wide[:rows]
        r_wide[:, cols] = wide[rows : 2 * rows]
        e_wide[:, cols] = wide[2 * rows : 2 * rows + 8]

    for g in range(GROUPS):
        pass_out[g] = e_wide[:, g * width : (g + 1) * width]
    pass_copies = []
    for o in others:
        copy = remote(pass_out.at[o], pass_in.at[r], pass_send.at[o], pass_recv.at[r], slab + o)
        copy.start()
        pass_copies.append(copy)
    pass_in[r] = pass_out[r]

    place = lax.broadcasted_iota(jnp.int32, (rows, rows + 16), 1)
    place = jnp.where(place < rows, place, place - (rows + 16))
    behind = lax.broadcasted_iota(jnp.int32, (rows, rows + 16), 0) - place
    shift = jnp.concatenate(
        [jnp.where((behind == taps - 1 - t) & tap_same[t], 1.0, 0.0) for t in range(taps - 1)], axis=0
    ).astype(bf16)
    loads[1].wait()
    loads[2].wait()
    rim_copy.wait()

    def conv(start, size):
        cols = pl.ds(start, size)
        moved = dot(shift, ext[:, cols])
        acc = cb_s[:, cols] + cw_s[taps - 1 : taps, cols] * ext[:rows, cols].astype(f32)
        for t in range(taps - 1):
            acc = acc + cw_s[t : t + 1, cols] * moved[t * rows : (t + 1) * rows]
        return (acc * sigmoid(acc)).astype(bf16)

    bs = conv(inner, GROUPS * state)
    cs = conv(inner + GROUPS * state, GROUPS * state)
    mask = below & (own == own_row)
    to_end = own == last
    from_prior = own == prior
    for g in range(GROUPS):
        b_g = bs[:, g * state : (g + 1) * state]
        c_g = cs[:, g * state : (g + 1) * state]
        raw_score = lax.dot_general(c_g, b_g, (((1,), (1,)), ((), ())), preferred_element_type=f32)
        score[g] = jnp.where(mask, raw_score, 0.0).astype(bf16)
        c_in[g] = jnp.where(from_prior, c_g.astype(f32), 0.0).astype(bf16)
        b_end[g] = jnp.where(to_end, b_g.astype(f32), 0.0).T.astype(bf16)

    def local(g, dst):
        def body(i, _):
            at = pl.multiple_of(g * width + i * tile, tile)
            cols = pl.ds(at, tile)
            x = conv(at, tile)
            x_s[:, cols] = x
            xs = (x.astype(f32) * r_wide[:, cols]).astype(bf16)
            xs_s[:, cols] = xs
            made = dot(b_end[g], xs) * e_wide[0:1, cols]
            dst[:, pl.ds(pl.multiple_of(i * tile, tile), tile)] = made.astype(bf16)
            return 0

        lax.fori_loop(0, width // tile, body, 0, unroll=True)

    a_copies = []
    for o in others:
        local(o, a_out.at[o])
        copy = remote(a_out.at[o], a_in.at[r], a_send.at[o], a_recv.at[r], slab + o)
        copy.start()
        a_copies.append(copy)
    local(r, a_in.at[r])

    def inside(i, _):
        g = i // (width // tile)
        cols = pl.ds(pl.multiple_of(i * tile, tile), tile)
        part_s[:, cols] = l_wide[:, cols] * dot(score[g], xs_s[:, cols]) + e_wide[2:3, cols] * x_s[:, cols].astype(f32)
        gate = gate_s[:, cols].astype(f32)
        sg_s[:, cols] = gate * sigmoid(gate)
        return 0

    loads[3].wait()
    lax.fori_loop(0, inner // tile, inside, 0, unroll=True)

    for o in others:
        remote(pass_out.at[o], pass_in.at[o], pass_send.at[o], pass_recv.at[o], slab + o).wait_recv()
        remote(a_out.at[o], a_in.at[o], a_send.at[o], a_recv.at[o], slab + o).wait_recv()

    def chain(i, p):
        at = i * PIECES + p
        return remote(ch_out.at[at], ch_in.at[at], ch_send.at[at], ch_recv.at[at], up)

    def emit(p):
        cols = slice(p * piece, (p + 1) * piece)
        total = a_in[0, :, cols].astype(f32)
        for k in range(1, GROUPS):
            total = total * pass_in[k, 1:2, cols] + a_in[k, :, cols].astype(f32)
        ch_out[p] = total.astype(bf16)

        @pl.when(z < nz - 1)
        def _():
            chain(0, p).start()

    def gather(i, p):
        @pl.when(z == 0)
        def _():
            ch_in[i * PIECES + p] = jnp.zeros((state, piece), bf16)

        @pl.when(z > 0)
        def _():
            chain(i, p).wait_recv()

        if i + 1 < reach:
            cols = slice(p * piece, (p + 1) * piece)
            whole = pass_in[0, 1:2, cols]
            for k in range(1, GROUPS):
                whole = whole * pass_in[k, 1:2, cols]
            ch_out[(i + 1) * PIECES + p] = (ch_in[i * PIECES + p].astype(f32) * whole).astype(bf16)

            @pl.when(z < nz - 1)
            def _():
                chain(i + 1, p).start()

    for p in range(PIECES):
        emit(p)
    for i in range(reach - 1):
        for p in range(PIECES):
            gather(i, p)
    for p in range(PIECES):
        gather(reach - 1, p)
        cols = slice(p * piece, (p + 1) * piece)
        held = ch_in[p].astype(f32)
        for i in range(1, reach):
            held = held + ch_in[i * PIECES + p].astype(f32)
        for k in range(GROUPS):
            s_out[k, p] = held.astype(bf16)
            if k + 1 < GROUPS:
                held = held * pass_in[k, 1:2, cols] + a_in[k, :, cols].astype(f32)
        for o in others:
            remote(
                s_out.at[o, p], s_in.at[r, p], s_send.at[o * PIECES + p], s_recv.at[r * PIECES + p], slab + o
            ).start()
        s_in[r, p] = s_out[r, p]

    ones = jnp.where(
        lax.broadcasted_iota(jnp.int32, (tile, tile), 0) // head_dim
        == lax.broadcasted_iota(jnp.int32, (tile, tile), 1) // head_dim,
        1.0 / head_dim,
        0.0,
    ).astype(bf16)

    def finish(g, p):
        def body(i, _):
            cols = pl.ds(pl.multiple_of(g * width + p * piece + i * tile, tile), tile)
            arrived = s_in[g, p, :, pl.ds(pl.multiple_of(i * tile, tile), tile)]
            both = part_s[:, cols] + l_wide[:, cols] * dot(c_in[g], arrived)
            gated = both * sg_s[:, cols]
            mean = dot((gated * gated).astype(bf16), ones)
            out_ref[:, cols] = (gated * lax.rsqrt(mean + epsilon) * norm_ref[:, cols]).astype(bf16)
            return 0

        lax.fori_loop(0, piece // tile, body, 0, unroll=True)

    for p in range(PIECES):
        finish(r, p)
        for o in [others[2], others[0], others[1]]:
            remote(
                s_out.at[o, p], s_in.at[o, p], s_send.at[o * PIECES + p], s_recv.at[o * PIECES + p], slab + o
            ).wait_recv()
            finish(o, p)

    for copy in pass_copies + a_copies:
        copy.wait_send()
    for p in range(PIECES):
        for o in others:
            remote(
                s_out.at[o, p], s_in.at[r, p], s_send.at[o * PIECES + p], s_recv.at[r * PIECES + p], slab + o
            ).wait_send()

        for i in range(reach):

            @pl.when(z < nz - 1)
            def _():
                chain(i, p).wait_send()


def on_device(
    n_seq,
    mixer_in,
    gate_in,
    step_raw,
    step_bias,
    rate_log,
    conv_weight,
    conv_bias,
    skip_gain,
    norm_gain,
    doc_lengths,
):
    rows, ch = mixer_in.shape
    inner = gate_in.shape[1]
    heads = step_raw.shape[1]
    state = (ch - inner) // (2 * GROUPS)
    width = inner // GROUPS
    piece = width // PIECES
    vmem = pl.BlockSpec(memory_space=pltpu.VMEM)
    hbm = pl.BlockSpec(memory_space=pltpu.HBM)
    reach = nz_half(n_seq)
    dma = pltpu.SemaphoreType.DMA
    return pl.pallas_call(
        functools.partial(kernel, n_seq),
        out_shape=jax.ShapeDtypeStruct((rows, inner), bf16),
        in_specs=[hbm] * 10,
        out_specs=vmem,
        scratch_shapes=[
            pltpu.VMEM((rows + 16, ch), bf16),
            pltpu.VMEM((rows, inner), bf16),
            pltpu.VMEM(conv_weight.shape, f32),
            pltpu.VMEM((1, ch), f32),
            pltpu.SMEM(doc_lengths.shape, jnp.int32),
            pltpu.VMEM(step_raw.shape, bf16),
            pltpu.VMEM((1, heads), f32),
            pltpu.VMEM((1, heads), f32),
            pltpu.VMEM((1, heads), f32),
            pltpu.VMEM((1, inner), f32),
            pltpu.VMEM((rows, inner), f32),
            pltpu.VMEM((rows, inner), f32),
            pltpu.VMEM((8, inner), f32),
            pltpu.VMEM((GROUPS, 8, width), f32),
            pltpu.VMEM((GROUPS, 8, width), f32),
            pltpu.VMEM((GROUPS, state, rows), bf16),
            pltpu.VMEM((GROUPS, rows, rows), bf16),
            pltpu.VMEM((GROUPS, rows, state), bf16),
            pltpu.VMEM((rows, inner), bf16),
            pltpu.VMEM((rows, inner), bf16),
            pltpu.VMEM((rows, inner), f32),
            pltpu.VMEM((rows, inner), f32),
            pltpu.VMEM((GROUPS, state, width), bf16),
            pltpu.VMEM((GROUPS, state, width), bf16),
            pltpu.VMEM((reach * PIECES, state, piece), bf16),
            pltpu.VMEM((reach * PIECES, state, piece), bf16),
            pltpu.VMEM((GROUPS, PIECES, state, piece), bf16),
            pltpu.VMEM((GROUPS, PIECES, state, piece), bf16),
            dma((10,)),
            dma((2,)),
            dma((GROUPS,)),
            dma((GROUPS,)),
            dma((GROUPS,)),
            dma((GROUPS,)),
            dma((reach * PIECES,)),
            dma((reach * PIECES,)),
            dma((GROUPS * PIECES,)),
            dma((GROUPS * PIECES,)),
        ],
        compiler_params=pltpu.CompilerParams(
            collective_id=0, has_side_effects=True, vmem_limit_bytes=62 * 1024 * 1024
        ),
        cost_estimate=pl.CostEstimate(flops=100_000_000, bytes_accessed=2_000_000, transcendentals=1_000_000),
    )(
        doc_lengths,
        mixer_in,
        gate_in,
        step_raw,
        step_bias,
        rate_log,
        conv_weight,
        conv_bias,
        skip_gain,
        norm_gain,
    )


def solution(mesh):
    return jax.shard_map(
        functools.partial(on_device, mesh.shape["seq"]),
        mesh=mesh,
        in_specs=(
            P(("groups", "seq"), None),
            P(("groups", "seq"), None),
            P(("groups", "seq"), None),
            P(),
            P(),
            P(),
            P(),
            P(),
            P(),
            P("groups"),
        ),
        out_specs=P(("groups", "seq"), None),
        check_vma=False,
    )
```

```python
import functools

import jax
import jax.numpy as jnp
from jax import lax
from jax.experimental import pallas as pl
from jax.experimental.pallas import tpu as pltpu
from jax.sharding import PartitionSpec as P

GROUPS = 4
PIECES = 4
epsilon = 1e-05
f32 = jnp.float32
bf16 = jnp.bfloat16


def dot(a, b):
    return jnp.dot(a, b, preferred_element_type=f32)


def halves(v):
    high = v.astype(bf16)
    return high, (v - high.astype(f32)).astype(bf16)


def sigmoid(v):
    return 0.5 * jnp.tanh(0.5 * v) + 0.5


def nz_half(n_seq):
    return max(1, n_seq // GROUPS // 2)


def kernel(
    n_seq,
    doc_hbm,
    mix_ref,
    gate_ref,
    raw_hbm,
    bias_hbm,
    rate_hbm,
    cw_ref,
    cb_ref,
    skip_hbm,
    norm_hbm,
    out_ref,
    ext,
    gate_s,
    cw_s,
    cb_s,
    doc_ref,
    raw_ref,
    bias_ref,
    rate_ref,
    skip_ref,
    norm_ref,
    l_wide,
    r_wide,
    e_wide,
    pass_out,
    pass_in,
    b_end,
    score,
    c_in,
    x_s,
    xs_s,
    part_s,
    sg_s,
    a_out,
    a_in,
    ch_out,
    ch_in,
    s_out,
    s_in,
    load_sem,
    rim_sem,
    pass_send,
    pass_recv,
    a_send,
    a_recv,
    ch_send,
    ch_recv,
    s_send,
    s_recv,
):
    rows, ch = mix_ref.shape
    inner = gate_ref.shape[1]
    heads = raw_hbm.shape[1]
    head_dim = inner // heads
    state = (ch - inner) // (2 * GROUPS)
    width = inner // GROUPS
    taps = cw_ref.shape[0]
    docs = doc_hbm.shape[0]
    tile = min(256, width)
    piece = width // PIECES
    reach = nz_half(n_seq)

    me = lax.axis_index("seq")
    r = lax.rem(me, GROUPS)
    z = me // GROUPS
    nz = n_seq // GROUPS
    slab = z * GROUPS
    others = [lax.rem(r + 2, 4), 3 - r, r + 1 - 2 * lax.rem(r, 2)]
    nxt, prv = lax.rem(me + 1, n_seq), lax.rem(me + n_seq - 1, n_seq)
    up, down = lax.rem(me + GROUPS, n_seq), lax.rem(me + n_seq - GROUPS, n_seq)

    loads = [
        pltpu.make_async_copy(mix_ref, ext.at[pl.ds(0, rows)], load_sem.at[0]),
        pltpu.make_async_copy(cw_ref, cw_s, load_sem.at[1]),
        pltpu.make_async_copy(cb_ref, cb_s.at[0], load_sem.at[2]),
        pltpu.make_async_copy(gate_ref, gate_s, load_sem.at[3]),
        pltpu.make_async_copy(doc_hbm, doc_ref, load_sem.at[4]),
        pltpu.make_async_copy(raw_hbm, raw_ref, load_sem.at[5]),
        pltpu.make_async_copy(bias_hbm, bias_ref.at[0], load_sem.at[6]),
        pltpu.make_async_copy(rate_hbm, rate_ref.at[0], load_sem.at[7]),
        pltpu.make_async_copy(skip_hbm, skip_ref.at[0], load_sem.at[8]),
        pltpu.make_async_copy(norm_hbm, norm_ref.at[0], load_sem.at[9]),
    ]
    for load in loads:
        load.start()
    barrier = pltpu.get_barrier_semaphore()
    near = [slab + o for o in others] + [nxt, prv, up, down]
    for d in near:
        pl.semaphore_signal(barrier, inc=1, device_id={"seq": d}, device_id_type=pl.DeviceIdType.MESH)

    def remote(src, dst, send, recv, to):
        return pltpu.make_async_remote_copy(
            src_ref=src,
            dst_ref=dst,
            send_sem=send,
            recv_sem=recv,
            device_id={"seq": to},
            device_id_type=pl.DeviceIdType.MESH,
        )

    pl.semaphore_wait(barrier, len(near))
    loads[0].wait()
    rim_copy = remote(
        ext.at[pl.ds(rows - 16, 16)], ext.at[pl.ds(rows, 16)], rim_sem.at[0], rim_sem.at[1], nxt
    )
    rim_copy.start()

    for load in loads[4:]:
        load.wait()

    ends = []
    total = jnp.int32(0)
    for d in range(docs):
        total = total + doc_ref[d]
        ends.append(total)

    def doc_of(pos):
        inside = jnp.zeros(pos.shape, jnp.int32)
        for end in ends:
            inside = inside + jnp.where(pos >= end, 1, 0)
        return jnp.where(pos >= 0, inside, -1)

    first = me * rows
    pos_col = first + lax.broadcasted_iota(jnp.int32, (rows, 1), 0)
    own = doc_of(pos_col)
    own_row = doc_of(first + lax.broadcasted_iota(jnp.int32, (1, rows), 1))
    prior = doc_of(jnp.full((1, 1), first - 1, jnp.int32))
    last = doc_of(jnp.full((1, 1), first + rows - 1, jnp.int32))
    tap_same = [doc_of(pos_col - (taps - 1 - t)) == own for t in range(taps - 1)]

    step = jnp.log(1.0 + jnp.exp(raw_ref[...].astype(f32) + bias_ref[...]))
    fall = -jnp.exp(rate_ref[...]) * step
    below = lax.broadcasted_iota(jnp.int32, (rows, rows), 0) >= lax.broadcasted_iota(jnp.int32, (rows, rows), 1)
    logs = jnp.dot(below.astype(f32), fall, preferred_element_type=f32, precision=lax.Precision.HIGHEST)
    l_small = jnp.exp(logs)
    r_small = jnp.exp(-logs) * step
    e_small = l_small[rows - 1 : rows, :]
    p_small = jnp.where(last == prior, e_small, 0.0)

    low8 = jnp.concatenate([e_small, p_small, skip_ref[...], jnp.zeros((5, heads), f32)], axis=0)
    stack = jnp.concatenate([l_small, r_small, low8, jnp.zeros((8, heads), f32)], axis=0)
    split = jnp.concatenate(halves(stack), axis=1)
    gap = lax.rem(lax.broadcasted_iota(jnp.int32, (2 * heads, tile), 0), heads) - (
        lax.broadcasted_iota(jnp.int32, (2 * heads, tile), 1) // head_dim
    )
    for c in range(inner // tile):
        wide = dot(split, jnp.where(gap == c * (tile // head_dim), 1.0, 0.0).astype(bf16))
        cols = slice(c * tile, (c + 1) * tile)
        l_wide[:, cols] = wide[:rows]
        r_wide[:, cols] = wide[rows : 2 * rows]
        e_wide[:, cols] = wide[2 * rows : 2 * rows + 8]

    for g in range(GROUPS):
        pass_out[g] = e_wide[:, g * width : (g + 1) * width]
    pass_copies = []
    for o in others:
        copy = remote(pass_out.at[o], pass_in.at[r], pass_send.at[o], pass_recv.at[r], slab + o)
        copy.start()
        pass_copies.append(copy)
    pass_in[r] = pass_out[r]

    place = lax.broadcasted_iota(jnp.int32, (rows, rows + 16), 1)
    place = jnp.where(place < rows, place, place - (rows + 16))
    behind = lax.broadcasted_iota(jnp.int32, (rows, rows + 16), 0) - place
    shift = jnp.concatenate(
        [jnp.where((behind == taps - 1 - t) & tap_same[t], 1.0, 0.0) for t in range(taps - 1)], axis=0
    ).astype(bf16)
    loads[1].wait()
    loads[2].wait()
    rim_copy.wait()

    def conv(start, size):
        cols = pl.ds(start, size)
        moved = dot(shift, ext[:, cols])
        acc = cb_s[:, cols] + cw_s[taps - 1 : taps, cols] * ext[:rows, cols].astype(f32)
        for t in range(taps - 1):
            acc = acc + cw_s[t : t + 1, cols] * moved[t * rows : (t + 1) * rows]
        return (acc * sigmoid(acc)).astype(bf16)

    bs = conv(inner, GROUPS * state)
    cs = conv(inner + GROUPS * state, GROUPS * state)
    mask = below & (own == own_row)
    to_end = own == last
    from_prior = own == prior
    for g in range(GROUPS):
        b_g = bs[:, g * state : (g + 1) * state]
        c_g = cs[:, g * state : (g + 1) * state]
        raw_score = lax.dot_general(c_g, b_g, (((1,), (1,)), ((), ())), preferred_element_type=f32)
        score[g] = jnp.where(mask, raw_score, 0.0).astype(bf16)
        c_in[g] = jnp.where(from_prior, c_g.astype(f32), 0.0).astype(bf16)
        b_end[g] = jnp.where(to_end, b_g.astype(f32), 0.0).T.astype(bf16)

    def local(g, dst):
        def body(i, _):
            at = pl.multiple_of(g * width + i * tile, tile)
            cols = pl.ds(at, tile)
            x = conv(at, tile)
            x_s[:, cols] = x
            xs = (x.astype(f32) * r_wide[:, cols]).astype(bf16)
            xs_s[:, cols] = xs
            made = dot(b_end[g], xs) * e_wide[0:1, cols]
            dst[:, pl.ds(pl.multiple_of(i * tile, tile), tile)] = made.astype(bf16)
            return 0

        lax.fori_loop(0, width // tile, body, 0, unroll=True)

    a_copies = []
    for o in others:
        local(o, a_out.at[o])
        copy = remote(a_out.at[o], a_in.at[r], a_send.at[o], a_recv.at[r], slab + o)
        copy.start()
        a_copies.append(copy)
    local(r, a_in.at[r])

    def inside(i, _):
        g = i // (width // tile)
        cols = pl.ds(pl.multiple_of(i * tile, tile), tile)
        part_s[:, cols] = l_wide[:, cols] * dot(score[g], xs_s[:, cols]) + e_wide[2:3, cols] * x_s[:, cols].astype(f32)
        gate = gate_s[:, cols].astype(f32)
        sg_s[:, cols] = gate * sigmoid(gate)
        return 0

    loads[3].wait()
    lax.fori_loop(0, inner // tile, inside, 0, unroll=True)

    for o in others:
        remote(pass_out.at[o], pass_in.at[o], pass_send.at[o], pass_recv.at[o], slab + o).wait_recv()
        remote(a_out.at[o], a_in.at[o], a_send.at[o], a_recv.at[o], slab + o).wait_recv()

    def chain(i, p):
        at = i * PIECES + p
        return remote(ch_out.at[at], ch_in.at[at], ch_send.at[at], ch_recv.at[at], up)

    def emit(p):
        cols = slice(p * piece, (p + 1) * piece)
        total = a_in[0, :, cols].astype(f32)
        for k in range(1, GROUPS):
            total = total * pass_in[k, 1:2, cols] + a_in[k, :, cols].astype(f32)
        ch_out[p] = total.astype(bf16)

        @pl.when(z < nz - 1)
        def _():
            chain(0, p).start()

    def gather(i, p):
        @pl.when(z == 0)
        def _():
            ch_in[i * PIECES + p] = jnp.zeros((state, piece), bf16)

        @pl.when(z > 0)
        def _():
            chain(i, p).wait_recv()

        if i + 1 < reach:
            cols = slice(p * piece, (p + 1) * piece)
            whole = pass_in[0, 1:2, cols]
            for k in range(1, GROUPS):
                whole = whole * pass_in[k, 1:2, cols]
            ch_out[(i + 1) * PIECES + p] = (ch_in[i * PIECES + p].astype(f32) * whole).astype(bf16)

            @pl.when(z < nz - 1)
            def _():
                chain(i + 1, p).start()

    for p in range(PIECES):
        emit(p)
    for i in range(reach - 1):
        for p in range(PIECES):
            gather(i, p)
    for p in range(PIECES):
        gather(reach - 1, p)
        cols = slice(p * piece, (p + 1) * piece)
        held = ch_in[p].astype(f32)
        for i in range(1, reach):
            held = held + ch_in[i * PIECES + p].astype(f32)
        for k in range(GROUPS):
            s_out[k, p] = held.astype(bf16)
            if k + 1 < GROUPS:
                held = held * pass_in[k, 1:2, cols] + a_in[k, :, cols].astype(f32)
        for o in others:
            remote(
                s_out.at[o, p], s_in.at[r, p], s_send.at[o * PIECES + p], s_recv.at[r * PIECES + p], slab + o
            ).start()
        s_in[r, p] = s_out[r, p]

    ones = jnp.where(
        lax.broadcasted_iota(jnp.int32, (tile, tile), 0) // head_dim
        == lax.broadcasted_iota(jnp.int32, (tile, tile), 1) // head_dim,
        1.0 / head_dim,
        0.0,
    ).astype(bf16)

    def finish(g, p):
        def body(i, _):
            cols = pl.ds(pl.multiple_of(g * width + p * piece + i * tile, tile), tile)
            arrived = s_in[g, p, :, pl.ds(pl.multiple_of(i * tile, tile), tile)]
            both = part_s[:, cols] + l_wide[:, cols] * dot(c_in[g], arrived)
            gated = both * sg_s[:, cols]
            mean = dot((gated * gated).astype(bf16), ones)
            out_ref[:, cols] = (gated * lax.rsqrt(mean + epsilon) * norm_ref[:, cols]).astype(bf16)
            return 0

        lax.fori_loop(0, piece // tile, body, 0, unroll=True)

    for p in range(PIECES):
        finish(r, p)
        for o in [others[2], others[0], others[1]]:
            remote(
                s_out.at[o, p], s_in.at[o, p], s_send.at[o * PIECES + p], s_recv.at[o * PIECES + p], slab + o
            ).wait_recv()
            finish(o, p)

    for copy in pass_copies + a_copies:
        copy.wait_send()
    for p in range(PIECES):
        for o in others:
            remote(
                s_out.at[o, p], s_in.at[r, p], s_send.at[o * PIECES + p], s_recv.at[r * PIECES + p], slab + o
            ).wait_send()

        for i in range(reach):

            @pl.when(z < nz - 1)
            def _():
                chain(i, p).wait_send()


def on_device(
    n_seq,
    mixer_in,
    gate_in,
    step_raw,
    step_bias,
    rate_log,
    conv_weight,
    conv_bias,
    skip_gain,
    norm_gain,
    doc_lengths,
):
    rows, ch = mixer_in.shape
    inner = gate_in.shape[1]
    heads = step_raw.shape[1]
    state = (ch - inner) // (2 * GROUPS)
    width = inner // GROUPS
    piece = width // PIECES
    vmem = pl.BlockSpec(memory_space=pltpu.VMEM)
    hbm = pl.BlockSpec(memory_space=pltpu.HBM)
    reach = nz_half(n_seq)
    dma = pltpu.SemaphoreType.DMA
    return pl.pallas_call(
        functools.partial(kernel, n_seq),
        out_shape=jax.ShapeDtypeStruct((rows, inner), bf16),
        in_specs=[hbm] * 10,
        out_specs=vmem,
        scratch_shapes=[
            pltpu.VMEM((rows + 16, ch), bf16),
            pltpu.VMEM((rows, inner), bf16),
            pltpu.VMEM(conv_weight.shape, f32),
            pltpu.VMEM((1, ch), f32),
            pltpu.SMEM(doc_lengths.shape, jnp.int32),
            pltpu.VMEM(step_raw.shape, bf16),
            pltpu.VMEM((1, heads), f32),
            pltpu.VMEM((1, heads), f32),
            pltpu.VMEM((1, heads), f32),
            pltpu.VMEM((1, inner), f32),
            pltpu.VMEM((rows, inner), f32),
            pltpu.VMEM((rows, inner), f32),
            pltpu.VMEM((8, inner), f32),
            pltpu.VMEM((GROUPS, 8, width), f32),
            pltpu.VMEM((GROUPS, 8, width), f32),
            pltpu.VMEM((GROUPS, state, rows), bf16),
            pltpu.VMEM((GROUPS, rows, rows), bf16),
            pltpu.VMEM((GROUPS, rows, state), bf16),
            pltpu.VMEM((rows, inner), bf16),
            pltpu.VMEM((rows, inner), bf16),
            pltpu.VMEM((rows, inner), f32),
            pltpu.VMEM((rows, inner), f32),
            pltpu.VMEM((GROUPS, state, width), bf16),
            pltpu.VMEM((GROUPS, state, width), bf16),
            pltpu.VMEM((reach * PIECES, state, piece), bf16),
            pltpu.VMEM((reach * PIECES, state, piece), bf16),
            pltpu.VMEM((GROUPS, PIECES, state, piece), bf16),
            pltpu.VMEM((GROUPS, PIECES, state, piece), bf16),
            dma((10,)),
            dma((2,)),
            dma((GROUPS,)),
            dma((GROUPS,)),
            dma((GROUPS,)),
            dma((GROUPS,)),
            dma((reach * PIECES,)),
            dma((reach * PIECES,)),
            dma((GROUPS * PIECES,)),
            dma((GROUPS * PIECES,)),
        ],
        compiler_params=pltpu.CompilerParams(
            collective_id=0, has_side_effects=True, vmem_limit_bytes=62 * 1024 * 1024
        ),
        cost_estimate=pl.CostEstimate(flops=100_000_000, bytes_accessed=2_000_000, transcendentals=1_000_000),
    )(
        doc_lengths,
        mixer_in,
        gate_in,
        step_raw,
        step_bias,
        rate_log,
        conv_weight,
        conv_bias,
        skip_gain,
        norm_gain,
    )


def solution(mesh):
    return jax.shard_map(
        functools.partial(on_device, mesh.shape["seq"]),
        mesh=mesh,
        in_specs=(
            P(("groups", "seq"), None),
            P(("groups", "seq"), None),
            P(("groups", "seq"), None),
            P(),
            P(),
            P(),
            P(),
            P(),
            P(),
            P("groups"),
        ),
        out_specs=P(("groups", "seq"), None),
        check_vma=False,
    )
```
